512 devices in a mesh: pair: 16 (over x, y), intg: 32 (over z, core).
Axes of the slice: x: 4, y: 4, z: 16, core: 2. Of those that a mesh axis runs over, the one named last changes fastest.
Arguments:
- amplitudes: bfloat16 [2048, 12288], P('pair', 'intg'), may hold values from -6 to 6
- integrals: bfloat16 [32, 32, 5, 128, 128], P('intg', None, None, 'pair'), may hold values from -0.0390625 to 0.0390625
- cd_index: int32 [32, 32, 5], replicated, may hold values from 0 to 2
- ab_index: int32 [32, 32, 5], replicated, may hold values from 0 to 31
- owner_map: int32 [32], replicated, may hold values from 0 to 31, each once
Outputs:
- residual: bfloat16 [2048, 4096], P('pair', 'intg')
The draws below stay inside these ranges and needn't reach their ends.
Inputs may be any that keep to these rules, and one draw needn't show every extreme that they name: owner_map is a permutation of the residual tile columns.
All inputs are finite; a program needn't handle non-finite values.
Results may differ from the reference program's by a relative error of at most 0.00175.
Values may be sent and summed in bfloat16 or wider, within the bound.
A program may use at most 64 MiB of HBM per device.

```python
import math
import jax
import jax.numpy as jnp
import numpy as np
from jax import lax

TILE = 128
KT_DEV = 3
CAP = 5
PAIRS = 2048
KT_TILES = 96
RES_TILES = 32
N_INTG = 32


def touch_ends(values, stream_key, least, largest):
    longest = values.shape.index(max(values.shape))
    spots = []
    for shift in (0, 1):
        where = [jax.random.randint(jax.random.fold_in(stream_key, axis), (), 0, length) for axis, length in enumerate(values.shape)]
        where[longest] = (where[longest] + shift) % values.shape[longest]
        spots.append(tuple(where))
    return values.at[spots[0]].set(least).at[spots[1]].set(largest)


def steps_of(own_key, extent, pieces, least, top_value):
    level = 1.0
    for axis_at, blocks in pieces:
        draws = jax.random.uniform(jax.random.fold_in(jax.random.fold_in(own_key, 6), axis_at), (blocks,), jnp.float32, least / len(pieces), top_value / len(pieces))
        level = level * jnp.repeat(jnp.exp(draws), extent[axis_at] // blocks).reshape((-1,) + (1,) * (len(extent) - 1 - axis_at))
    return level


def rank_bounds(count, skew):
    loads = [(1 << 20) // math.isqrt(rank ** skew) + 1 for rank in range(1, count + 1)]
    spread = 1 + sum(loads) // (1 << 30)
    return np.cumsum(np.array([max(1, weight // spread) for weight in loads]))


def skewed_ids(own_key, shape, count, slope):
    listing = rank_bounds(count, slope)
    lot = jax.random.randint(jax.random.fold_in(own_key, 1), shape, 0, int(listing[count - 1]))
    rank = jnp.searchsorted(jnp.asarray(listing, jnp.int32), lot, side="right")
    return jax.random.permutation(jax.random.fold_in(own_key, 2), count)[rank].astype(jnp.int32)


def centred(stream_key, dims, deviation, bound, split=(), held_as=jnp.bfloat16):
    values = jax.random.normal(stream_key, dims, jnp.float32) * deviation
    if len(split) > 0:
        values = steps_of(stream_key, dims, split, -0.22, 0.18) * values
    return jnp.clip(values, min=-bound, max=bound).astype(held_as)


def setup_inputs(seed: int = 0) -> dict:
    streams_of = jax.random.split(jax.random.key(seed), 6)
    amplitudes = centred(streams_of[0], (PAIRS, KT_TILES * TILE), 1.0, 6.0, ((0, 16), (1, 32)))
    integrals = centred(streams_of[1], (N_INTG, N_INTG, CAP, TILE, TILE), (N_INTG * CAP * TILE) ** -0.5, 0.0390625, ((0, 32), (3, 16)))
    cd_index = touch_ends(jax.random.randint(streams_of[2], (N_INTG, N_INTG, CAP), 0, KT_DEV), jax.random.fold_in(streams_of[2], 1), 0, KT_DEV - 1).astype(jnp.int32)
    ab_index = touch_ends(skewed_ids(streams_of[3], (N_INTG, N_INTG, CAP), RES_TILES, 1), jax.random.fold_in(streams_of[3], 3), 0, RES_TILES - 1).astype(jnp.int32)
    owner_map = jax.random.permutation(streams_of[4], RES_TILES).astype(jnp.int32)
    return {"amplitudes": amplitudes, "integrals": integrals, "cd_index": cd_index, "ab_index": ab_index, "owner_map": owner_map}


def reference(amplitudes, integrals, cd_index, ab_index, owner_map):
    tile_size = integrals.shape[-1]
    group_size = integrals.shape[0]
    sources = integrals.reshape(-1, tile_size, tile_size).astype(jnp.float32)
    holders = jnp.arange(group_size, dtype=jnp.int32)[None, :, None]
    column_index = (holders * KT_DEV + cd_index).reshape(-1).astype(jnp.int32)
    inverse = jnp.zeros((RES_TILES,), jnp.int32).at[owner_map].set(jnp.arange(RES_TILES, dtype=jnp.int32))
    block_index = inverse[ab_index.reshape(-1)].astype(jnp.int32)
    assembled = jnp.zeros((KT_TILES, RES_TILES, tile_size, tile_size), jnp.float32)
    assembled = assembled.at[column_index, block_index].add(sources)
    assembled = assembled.transpose(0, 2, 1, 3).reshape(KT_TILES * tile_size, RES_TILES * tile_size)
    result = jnp.dot(amplitudes.astype(jnp.float32), assembled, precision=lax.Precision.HIGHEST)
    return result.astype(jnp.bfloat16)
```

```python
import jax
import jax.numpy as jnp
from jax import lax
from jax.experimental import pallas as pl
from jax.experimental.pallas import tpu as pltpu
from jax.sharding import PartitionSpec as P

MESH = pl.DeviceIdType.MESH
NX, NY, NZ = 4, 4, 16
CORES = 2
T = 128
KT = 3
CAP = 5
NI = NZ * CORES
TILES = NI * CAP
ROWS = 8
SHARD = TILES * ROWS
HALF = SHARD // 2
QUARTER = HALF // 2
NP = NX * NY
RES = 32
FAR = NZ // 2
UNROLL = 2


def index_table(cd_index, ab_index, owner_map):
    position = lax.axis_index("intg")
    cd = lax.dynamic_index_in_dim(cd_index, position, 0, keepdims=False).reshape(-1)
    ab = lax.dynamic_index_in_dim(ab_index, position, 0, keepdims=False).reshape(-1)
    order = jnp.arange(TILES, dtype=jnp.int32)
    holder = order // CAP
    amp = (holder % CORES) * (NZ * KT) + (holder // CORES) * KT + cd
    slots = jnp.arange(RES, dtype=jnp.int32)
    slot = jnp.sum(jnp.where(owner_map[None, :] == ab[:, None], slots[None, :], 0), axis=1)
    key = slot * TILES + order
    rank = jnp.sum((key[None, :] < key[:, None]).astype(jnp.int32), axis=1)
    hit = rank[None, :] == order[:, None]
    perm = jnp.sum(jnp.where(hit, order[None, :], 0), axis=1)
    sorted_slot = jnp.sum(jnp.where(hit, slot[None, :], 0), axis=1)
    before = jnp.concatenate([jnp.full((1,), -1, jnp.int32), sorted_slot[:-1]])
    keep = (sorted_slot == before).astype(jnp.int32)
    upto = jnp.sum((slot[None, :] <= slots[:, None]).astype(jnp.int32), axis=1)
    used = jnp.any(slot[None, :] == slots[:, None], axis=1).astype(jnp.int32)
    last = jnp.maximum(upto - 1, 0)
    return jnp.concatenate([amp, perm, keep, last, used])


AMP, PERM, KEEP, LAST, USED = 0, TILES, 2 * TILES, 3 * TILES, 3 * TILES + RES


def kernel(
    table, amp_hbm, int_hbm, out_ref,
    gath, amps, prods, sums, own, cross, ring_in, ring_out,
    local_sem, xy_send, xy_recv, z_send, z_recv, c_send, c_recv,
    x_send, x_recv, r_send, r_recv,
):
    p = lax.axis_index("pair")
    g = lax.axis_index("intg")
    x, y = p // NY, p % NY
    z, core = g // CORES, g % CORES
    sib = 1 - core

    def at_x(d):
        return ((x + d + NX) % NX, y)

    def at_y(d):
        return (x, (y + d + NY) % NY)

    def z_at(d):
        return (z + d + 2 * NZ) % NZ

    def flat(xy):
        return xy[0] * NY + xy[1]

    def xy_dev(xy):
        return (flat(xy), g)

    def z_dev(d):
        return (p, z_at(d) * CORES + core)

    sib_dev = (p, z * CORES + sib)

    def remote(src, dst, ss, rs, to):
        return pltpu.make_async_remote_copy(
            src_ref=src, dst_ref=dst, send_sem=ss, recv_sem=rs, device_id=to, device_id_type=MESH
        )

    barrier = pltpu.get_barrier_semaphore()
    partners = [xy_dev(at_x(1)), xy_dev(at_x(-1)), xy_dev(at_y(1)), xy_dev(at_y(-1)), z_dev(1), z_dev(-1), sib_dev]
    for to in partners:
        pl.semaphore_signal(barrier, inc=1, device_id=to, device_id_type=MESH)

    own_copy = pltpu.make_async_copy(int_hbm, gath.at[p], local_sem.at[0])
    own_copy.start()
    amp_copies = []
    for q in range(KT):
        c = pltpu.make_async_copy(
            amp_hbm.at[:, pl.ds(q * T, T)], amps.at[core, z * KT + q], local_sem.at[1 + q]
        )
        c.start()
        amp_copies.append(c)
    pl.semaphore_wait(barrier, len(partners))

    xy_sends = []

    def place(h, da, db):
        ax, by = (da, db) if h == 0 else (db, da)
        return ((x + ax + NX) % NX, (y + by + NY) % NY)

    def rows_of(h, part):
        if part is None:
            return h * HALF, HALF
        return h * HALF + part * QUARTER, QUARTER

    def xy_copy(h, sem, who, to, part, own=False):
        start, count = rows_of(h, part)
        src = int_hbm if own else gath.at[flat(who)]
        return remote(
            src.at[pl.ds(start, count)], gath.at[flat(who), pl.ds(start, count)],
            xy_send.at[h, sem], xy_recv.at[h, sem], xy_dev(to),
        )

    def xy_start(h, sem, who, to, part, own=False):
        c = xy_copy(h, sem, who, to, part, own)
        c.start()
        xy_sends.append(c)

    def xy_wait(h, sem, who, part):
        xy_copy(h, sem, who, place(h, 0, 1), part).wait_recv()

    SHIFT = (0, -1, 1, 2)

    def first_own(h):
        me = place(h, 0, 0)
        xy_start(h, 0, me, place(h, 1, 0), None, True)
        xy_start(h, 1, me, place(h, -1, 0), None, True)

    def second(h, q, own=False):
        who = place(h, SHIFT[q], 0)
        xy_start(h, 4 + 4 * q, who, place(h, 0, 1), None, own)
        xy_start(h, 5 + 4 * q, who, place(h, 0, -1), None, own)

    def first_forward(h, side):
        who = place(h, -1 if side == 0 else 1, 0)
        xy_wait(h, side, who, None)
        xy_start(h, 2 + side, who, place(h, 1 if side == 0 else -1, 0), side)

    def first_far(h):
        who = place(h, 2, 0)
        xy_wait(h, 2, who, 0)
        xy_wait(h, 3, who, 1)

    def second_forward(h, q):
        for side in (0, 1):
            who = place(h, SHIFT[q], -1 if side == 0 else 1)
            xy_wait(h, 4 + 4 * q + side, who, None)
            xy_start(h, 6 + 4 * q + side, who, place(h, 0, 1 if side == 0 else -1), side)

    def second_far(h, q):
        who = place(h, SHIFT[q], 2)
        xy_wait(h, 6 + 4 * q, who, 0)
        xy_wait(h, 7 + 4 * q, who, 1)

    z_sends = []

    def shard(d):
        return amps.at[core, pl.ds(z_at(d) * KT, KT)]

    def z_start(way, step):
        d = -step if way == 0 else step
        c = remote(shard(d), shard(d), z_send.at[way, step], z_recv.at[way, step], z_dev(1 if way == 0 else -1))
        c.start()
        z_sends.append(c)

    def z_wait(way, step):
        d = -step - 1 if way == 0 else step + 1
        remote(shard(d), shard(d), z_send.at[way, step], z_recv.at[way, step], z_dev(1)).wait_recv()

    def to_sibling(d):
        remote(shard(d), shard(d), c_send, c_recv, sib_dev).start()

    def z_step(step):
        for way in (0, 1):
            steps = FAR if way == 0 else FAR - 1
            if step >= steps:
                continue
            z_wait(way, step)
            if step + 1 < steps:
                z_start(way, step + 1)
            to_sibling(-step - 1 if way == 0 else step + 1)

    for h in (0, 1):
        first_own(h)
    for c in amp_copies:
        c.wait()
    z_start(0, 0)
    z_start(1, 0)
    for h in (0, 1):
        second(h, 0, True)
    to_sibling(0)
    z_step(0)
    for h in (0, 1):
        for side in (0, 1):
            first_forward(h, side)
            second(h, 1 + side)
    z_step(1)
    z_step(2)
    for h in (0, 1):
        second_forward(h, 0)
    for h in (0, 1):
        first_far(h)
        second(h, 3)
    z_step(3)
    z_step(4)
    for h in (0, 1):
        second_forward(h, 1)
    z_step(5)
    for h in (0, 1):
        second_forward(h, 2)
    z_step(6)
    z_step(7)
    for h in (0, 1):
        second_forward(h, 3)
    own_copy.wait()
    remote(amps.at[core], amps.at[sib], c_send, c_recv, sib_dev).wait()
    for h in (0, 1):
        for q in range(4):
            second_far(h, q)
    for c in xy_sends + z_sends:
        c.wait_send()

    def products(step, carry):
        for k in range(UNROLL):
            u = step * UNROLL + k
            group = gath[:, pl.ds(pl.multiple_of(u * 2 * ROWS, 2 * ROWS), 2 * ROWS), :].astype(jnp.float32)
            for odd in (0, 1):
                tile = group[:, odd * ROWS : (odd + 1) * ROWS, :].reshape(T, T).astype(jnp.bfloat16)
                a = table[AMP + 2 * u + odd]
                prods[2 * u + odd] = jnp.dot(amps[a // (NZ * KT), a % (NZ * KT)], tile, preferred_element_type=jnp.float32)
        return carry

    lax.fori_loop(0, TILES // 2 // UNROLL, products, 0)

    def running(t, acc):
        acc = jnp.where(table[KEEP + t] > 0, acc, 0.0) + prods[table[PERM + t]]
        sums[t] = acc
        return acc

    lax.fori_loop(0, TILES, running, jnp.zeros((T, T), jnp.float32))

    def pick(r, carry):
        own[r] = jnp.where(table[USED + r] > 0, sums[table[LAST + r]], 0.0)
        return carry

    lax.fori_loop(0, RES, pick, 0)

    far_first = [FAR]
    for d in range(FAR - 1, 0, -1):
        far_first += [d, -d]
    far_first.append(0)
    x_sends = {}
    for n, d in enumerate(far_first):
        c = remote(own.at[z_at(d) * CORES + sib], cross.at[n], x_send.at[n], x_recv.at[n], sib_dev)
        c.start()
        x_sends[d] = c

    hrows = T // 2
    r_sends = []

    def ring(way, step, part):
        rows = pl.ds(part * hrows, hrows)
        return remote(
            ring_out.at[way, step, rows], ring_in.at[way, step, rows],
            r_send.at[way, step, part], r_recv.at[way, step, part], z_dev(1 if way == 0 else -1),
        )

    def total(d, part):
        rows = pl.ds(part * hrows, hrows)
        return own[z_at(d) * CORES + core, rows, :] + cross[far_first.index(d), rows, :]

    x_sends[FAR].wait()
    for way in (0, 1):
        ring_out[way, 0, way * hrows : (way + 1) * hrows, :] = total(FAR, way)
        c = ring(way, 0, way)
        c.start()
        r_sends.append(c)
    for step in range(1, FAR):
        for way in (0, 1):
            d = FAR - step if way == 0 else step - FAR
            x_sends[d].wait()
            for part in ((way, 1 - way) if step == 1 else (0, 1)):
                value = total(d, part)
                if step > 1 or part == way:
                    ring(way, step - 1, part).wait_recv()
                    value = value + ring_in[way, step - 1, part * hrows : (part + 1) * hrows, :]
                ring_out[way, step, part * hrows : (part + 1) * hrows, :] = value
                c = ring(way, step, part)
                c.start()
                r_sends.append(c)
    x_sends[0].wait()
    for part in (0, 1):
        value = total(0, part)
        for way in (0, 1):
            ring(way, FAR - 1, part).wait_recv()
            value = value + ring_in[way, FAR - 1, part * hrows : (part + 1) * hrows, :]
        out_ref[part * hrows : (part + 1) * hrows, :] = value.astype(jnp.bfloat16)
    for c in r_sends:
        c.wait_send()


def per_device(amplitudes, integrals, cd_index, ab_index, owner_map):
    table = index_table(cd_index, ab_index, owner_map)
    shard = integrals.reshape(SHARD, T)
    dma = pltpu.SemaphoreType.DMA
    return pl.pallas_call(
        kernel,
        out_shape=jax.ShapeDtypeStruct((T, T), jnp.bfloat16),
        in_specs=[
            pl.BlockSpec(memory_space=pltpu.SMEM),
            pl.BlockSpec(memory_space=pl.ANY),
            pl.BlockSpec(memory_space=pl.ANY),
        ],
        out_specs=pl.BlockSpec(memory_space=pltpu.VMEM),
        scratch_shapes=[
            pltpu.VMEM((NP, SHARD, T), jnp.bfloat16),
            pltpu.VMEM((CORES, NZ * KT, T, T), jnp.bfloat16),
            pltpu.VMEM((TILES, T, T), jnp.float32),
            pltpu.VMEM((TILES, T, T), jnp.float32),
            pltpu.VMEM((RES, T, T), jnp.float32),
            pltpu.VMEM((NZ, T, T), jnp.float32),
            pltpu.VMEM((2, FAR, T, T), jnp.float32),
            pltpu.VMEM((2, FAR, T, T), jnp.float32),
            dma((1 + KT,)),
            dma((2, 20)), dma((2, 20)),
            dma((2, FAR)), dma((2, FAR)),
            dma, dma,
            dma((NZ,)), dma((NZ,)),
            dma((2, FAR, 2)), dma((2, FAR, 2)),
        ],
        compiler_params=pltpu.CompilerParams(
            collective_id=0, has_side_effects=True, vmem_limit_bytes=52 * 1024 * 1024
        ),
        name="ladder",
    )(table, amplitudes, shard)


def solution(mesh):
    return jax.shard_map(
        per_device,
        mesh=mesh,
        in_specs=(P("pair", "intg"), P("intg", None, None, "pair", None), P(), P(), P()),
        out_specs=P("pair", "intg"),
        check_vma=False,
    )
```

```python
import jax
import jax.numpy as jnp
from jax import lax
from jax.experimental import pallas as pl
from jax.experimental.pallas import tpu as pltpu
from jax.sharding import PartitionSpec as P

MESH = pl.DeviceIdType.MESH
NX, NY, NZ = 4, 4, 16
CORES = 2
T = 128
KT = 3
CAP = 5
NI = NZ * CORES
TILES = NI * CAP
ROWS = 8
SHARD = TILES * ROWS
NP = NX * NY
RES = 32
FAR = NZ // 2
BATCHES = 2
BATCH_TILES = TILES // BATCHES
CHUNK = SHARD // BATCHES // 2
QUAD_TILES = BATCH_TILES // 2
PIECE = CHUNK // 2
QUAD = 4
SOON = 5
JUMP_SUM = 5
PARTS = 4
UNROLL = 2
VMEM = 60 * 1024 * 1024


def quad_of(z, batch, half):
    side = 2 * ((z % QUAD) // 2) - 1
    step = (0, side, -side, 2)[2 * batch + half]
    return (z // QUAD + step + QUAD) % QUAD


PERM, KEEP, LAST, USED, WHICH = 0, 1, 2, 3, 4
GROUPS = BATCHES * RES
WIDE = 256


def iota(shape, dim):
    return lax.broadcasted_iota(jnp.int32, shape, dim)


def inside(value, count):
    return jnp.minimum(jnp.maximum(value, 0), count - 1)


def place_table(table, cd, ab, owner, z, g):
    f32, bf16 = jnp.float32, jnp.bfloat16

    def dot(a, b, dims=((1,), (0,))):
        return lax.dot_general(a.astype(bf16), b.astype(bf16), (dims, ((), ())), preferred_element_type=f32)

    eye = iota((RES, RES), 0) == iota((RES, RES), 1)
    owners = jnp.sum(jnp.where(eye, owner[...].astype(f32), 0.0), axis=1, keepdims=True)
    quad = iota((1, NI), 1) // (QUAD * CORES)
    early = (quad == quad_of(z, 0, 0)) | (quad == quad_of(z, 0, 1))
    member = jnp.zeros((GROUPS, WIDE), f32)
    for s in range(CAP):
        hit = owners == ab[s, pl.ds(g, 1), :].astype(f32)
        both = jnp.concatenate([jnp.where(hit & early, 1.0, 0.0), jnp.where(hit & ~early, 1.0, 0.0)], axis=0)
        spread = jnp.where(iota((NI, WIDE), 1) == iota((NI, WIDE), 0) + s * NI, 1.0, 0.0)
        member = member + dot(both, spread)
    before = dot(member, jnp.where(iota((WIDE, WIDE), 0) < iota((WIDE, WIDE), 1), 1.0, 0.0))
    counts = jnp.sum(member, axis=1, keepdims=True)
    lower = jnp.where(iota((GROUPS, GROUPS), 1) < iota((GROUPS, GROUPS), 0), 1.0, 0.0)
    starts = dot(lower, jnp.broadcast_to(counts, (GROUPS, T)))[:, :1]
    rank = jnp.sum(member * (starts + before), axis=0, keepdims=True).astype(jnp.int32)
    lane = iota((WIDE, WIDE), 1)
    moved = jnp.where((iota((WIDE, WIDE), 0) == rank) & (lane < TILES), 1.0, 0.0)
    tile = iota((8, WIDE), 1) % NI * CAP + iota((8, WIDE), 1) // NI
    perm = dot(tile, moved, ((1,), (1,)))
    full = counts > 0.0
    first = (iota((GROUPS, WIDE), 1).astype(f32) == starts) & full
    same = iota((GROUPS, WIDE), 1) == iota((GROUPS, WIDE), 0)
    last = jnp.where(same, jnp.clip(starts + counts - 1.0, 0.0, TILES - 1.0), 0.0)
    top = TILES - 1.0
    table[PERM : PERM + 1, :] = jnp.minimum(perm[:1], top).astype(jnp.int32)
    table[KEEP : KEEP + 1, :] = 1 - jnp.max(jnp.where(first, 1.0, 0.0), axis=0, keepdims=True).astype(jnp.int32)
    table[LAST : LAST + 1, :] = jnp.sum(last, axis=0, keepdims=True).astype(jnp.int32)
    table[USED : USED + 1, :] = jnp.max(jnp.where(same & full, 1.0, 0.0), axis=0, keepdims=True).astype(jnp.int32)
    for s in range(CAP):
        table[WHICH + s : WHICH + s + 1, :NI] = cd[s, pl.ds(g, 1), :]


def kernel(
    cd_hbm, ab_hbm, owner, amp_hbm, int_hbm, out_ref,
    table, cd, ab, table_vmem, index_sem,
    gath, amps, stage, prods, sums, own, cross, ring_in, ring_out,
    own_sem, amp_sem, xy_send, xy_recv, z_send, z_recv, c_send, c_recv,
    x_send, x_recv, r_send, r_recv,
):
    p = lax.axis_index("pair")
    g = lax.axis_index("intg")
    x, y = p // NY, p % NY
    z, core = g // CORES, g % CORES
    sib = 1 - core

    def flat(xy):
        return xy[0] * NY + xy[1]

    def xy_dev(xy):
        return (flat(xy), g)

    def z_at(d):
        return (z + d + 2 * NZ) % NZ

    def z_dev(d):
        return (p, z_at(d) * CORES + core)

    sib_dev = (p, z * CORES + sib)

    def remote(src, dst, ss, rs, to):
        return pltpu.make_async_remote_copy(
            src_ref=src, dst_ref=dst, send_sem=ss, recv_sem=rs, device_id=to, device_id_type=MESH
        )

    def place(h, da, db):
        ax, by = (da, db) if h == 0 else (db, da)
        return ((x + ax + NX) % NX, (y + by + NY) % NY)

    barrier = pltpu.get_barrier_semaphore()
    partners = [xy_dev(place(h, d, 0)) for h in (0, 1) for d in (1, -1)] + [sib_dev]
    partners += [z_dev(1), z_dev(-1)]
    for to in partners:
        pl.semaphore_signal(barrier, inc=1, device_id=to, device_id_type=MESH)

    own_copy = pltpu.make_async_copy(int_hbm, gath.at[p], own_sem)
    own_copy.start()
    own_amps = amps.at[pl.ds(core * (NZ * KT) + z * KT, KT)]
    for q in range(KT):
        pltpu.make_async_copy(amp_hbm.at[:, pl.ds(q * T, T)], own_amps.at[q], amp_sem).start()
    index_copies = [
        pltpu.make_async_copy(cd_hbm, cd, index_sem.at[0]), pltpu.make_async_copy(ab_hbm, ab, index_sem.at[1])
    ]
    for c in index_copies:
        c.start()
    pl.semaphore_wait(barrier, len(partners))

    SHIFT = (0, -1, 1, 2)
    FIRST, FIRST_FAR, SECOND, SECOND_FAR = 0, 1, 2, 6

    def xy_start(b, h, sem, who, to, part=None, own=False):
        start, count = pl.multiple_of(quad_of(z, b, h) * CHUNK, CHUNK), CHUNK
        if part is not None:
            start, count = start + part * PIECE, PIECE
        src = int_hbm if own else gath.at[flat(who)]
        remote(
            src.at[pl.ds(start, count)], gath.at[flat(who), pl.ds(start, count)],
            xy_send, xy_recv.at[b, sem], xy_dev(to),
        ).start()

    def xy_wait(b, sem, chunks):
        if chunks * CHUNK > SHARD:
            some = gath.at[pl.ds(0, chunks * CHUNK // SHARD)]
        else:
            some = gath.at[0, pl.ds(0, chunks * CHUNK)]
        pltpu.make_async_copy(some, some, xy_recv.at[b, sem]).wait()

    def first_own(b):
        for h in (0, 1):
            for d in (1, -1):
                xy_start(b, h, FIRST, place(h, 0, 0), place(h, d, 0), own=True)

    def second(b, q, own=False):
        for h in (0, 1):
            for d in (1, -1):
                xy_start(b, h, SECOND + q, place(h, SHIFT[q], 0), place(h, 0, d), own=own)

    def first_forward(b):
        xy_wait(b, FIRST, 4)
        for h in (0, 1):
            for d in (1, -1):
                xy_start(b, h, FIRST_FAR, place(h, -d, 0), place(h, d, 0), part=(1 - d) // 2)
        second(b, 1)
        second(b, 2)

    def first_far(b):
        xy_wait(b, FIRST_FAR, 2)
        second(b, 3)

    def second_forward(b, q):
        xy_wait(b, SECOND + q, 4)
        for h in (0, 1):
            for d in (1, -1):
                xy_start(b, h, SECOND_FAR, place(h, SHIFT[q], -d), place(h, 0, d), part=(1 - d) // 2)

    def second_far(b):
        xy_wait(b, SECOND_FAR, 8)

    SIGN = (1, -1)

    def tiles_wait(sem, count):
        some = amps.at[pl.ds(0, count)]
        pltpu.make_async_copy(some, some, sem).wait()

    def shard(owner_core, d):
        return amps.at[pl.ds(owner_core * (NZ * KT) + z_at(d) * KT, KT)]

    def z_start(dist, q):
        for way in (0, 1):
            part = shard(core, -SIGN[way] * (dist - 1)).at[q]
            if dist == FAR:
                part = part.at[pl.ds(way * (T // 2), T // 2)]
            remote(part, part, z_send, z_recv.at[dist - 1, q], z_dev(SIGN[way])).start()

    def to_sibling(dist):
        for way in (0,) if dist in (0, FAR) else (0, 1):
            part = shard(core, SIGN[way] * dist)
            remote(part, part, c_send, c_recv.at[0 if dist <= SOON else 1], sib_dev).start()

    def from_sibling(late):
        tiles_wait(c_recv.at[late], KT * (2 * (FAR - SOON) - 1 if late else 1 + 2 * SOON))

    def z_take(dist, q):
        tiles_wait(z_recv.at[dist - 1, q], 1 if dist == FAR else 2)
        if dist < FAR:
            z_start(dist + 1, q)
        if q == KT - 1:
            to_sibling(dist)

    def products(b, first, count):
        def body(n, carry):
            at = jnp.where(n < QUAD, quad_of(z, b, 0), quad_of(z, b, 1)) * QUAD + n % QUAD
            slot = n % 2 * (CORES * KT)
            for c in range(CORES):
                stage[pl.ds(slot + c * KT, KT)] = amps[pl.ds(c * (NZ * KT) + at * KT, KT)]
            for k in range(CAP):
                rows = pl.ds(pl.multiple_of(at * (2 * CAP * ROWS) + k * 2 * ROWS, 2 * ROWS), 2 * ROWS)
                group = gath[:, rows, :].astype(jnp.float32)
                for odd in (0, 1):
                    tile = group[:, odd * ROWS : (odd + 1) * ROWS, :].reshape(T, T).astype(jnp.bfloat16)
                    m = 2 * k + odd
                    which = inside(table[WHICH + m % CAP, at * CORES + m // CAP], KT)
                    prods[at * (2 * CAP) + m] = jnp.dot(
                        stage[slot + m // CAP * KT + which], tile, preferred_element_type=jnp.float32
                    )
            return carry

        lax.fori_loop(first, first + count, body, 0)

    def running(b):
        def body(t, acc):
            acc = jnp.where(table[KEEP, t] > 0, acc, 0.0) + prods[inside(table[PERM, t], TILES)]
            sums[t] = acc
            return acc

        lax.fori_loop(b * BATCH_TILES, (b + 1) * BATCH_TILES, body, jnp.zeros((T, T), jnp.float32))

    def slot_sum(b, r):
        at = b * RES + r
        return jnp.where(table[USED, at] > 0, sums[inside(table[LAST, at], TILES)], 0.0)

    def pick(b):
        def body(r, carry):
            value = slot_sum(b, r)
            own[r] = value if b == 0 else own[r] + value
            return carry

        lax.fori_loop(0, RES, body, 0)

    to_scalars = pltpu.make_async_copy(table_vmem, table, index_sem.at[0])

    def make_table():
        for c in index_copies:
            c.wait()
        place_table(table_vmem, cd, ab, owner, z, g)
        to_scalars.start()

    def table_done():
        to_scalars.wait()

    tiles_wait(amp_sem, KT)
    z_start(1, 0)
    first_own(0)
    second(0, 0, True)
    z_start(1, 1)
    z_start(1, 2)
    make_table()
    z_take(1, 0)
    first_own(1)
    z_take(1, 1)
    z_take(1, 2)
    first_forward(0)
    z_take(2, 0)
    z_take(2, 1)
    first_forward(1)
    z_take(2, 2)
    z_take(3, 0)
    z_take(3, 1)
    to_sibling(0)
    z_take(3, 2)
    first_far(0)
    z_take(4, 0)
    second_forward(0, 2)
    second_forward(0, 1)
    z_take(4, 1)
    z_take(4, 2)
    first_far(1)
    z_take(5, 0)
    z_take(5, 1)
    second(1, 0, True)
    z_take(5, 2)
    z_take(6, 0)
    second_forward(0, 0)
    second_forward(0, 3)
    z_take(6, 1)
    second_forward(1, 1)
    z_take(6, 2)
    second_forward(1, 0)
    from_sibling(0)
    z_take(7, 0)
    second_forward(1, 2)
    second_far(0)
    own_copy.wait()
    table_done()
    products(0, 6, 2)
    second_forward(1, 3)
    z_take(7, 1)
    z_take(7, 2)
    products(0, 4, 2)
    z_take(8, 0)
    products(0, 0, 2)
    products(0, 2, 2)
    second_far(1)
    z_take(8, 1)
    z_take(8, 2)
    running(0)
    pick(0)
    from_sibling(1)
    products(1, 0, 8)
    running(1)
    pick(1)

    def both(dist):
        return (dist,) if dist in (0, FAR) else (dist, -dist)

    def at_cross(d):
        return FAR + d if d != FAR else 0

    def blocks_wait(ref, sem, count):
        some = ref.at[pl.ds(0, count)]
        pltpu.make_async_copy(some, some, sem).wait()

    def cross_start(dist):
        for d in both(dist):
            remote(own.at[z_at(d) * CORES + sib], cross.at[at_cross(d)], x_send, x_recv.at[dist], sib_dev).start()

    def cross_wait(dist):
        blocks_wait(cross, x_recv.at[dist], len(both(dist)))

    hrows = T // PARTS

    def ring_start(way, dist, part):
        rows = pl.ds(part * hrows, hrows)
        hop = JUMP_SUM if dist == JUMP_SUM else 1
        remote(
            ring_out.at[2 * dist - 2 + way, rows], ring_in.at[2 * dist - 2 + way, rows],
            r_send, r_recv.at[dist - 1, part], z_dev(SIGN[way] * hop),
        ).start()

    def ring_wait(dist, part):
        some = ring_in.at[0, pl.ds(0, 2 * hrows if dist != FAR else hrows)]
        pltpu.make_async_copy(some, some, r_recv.at[dist - 1, part]).wait()

    def total(d, part):
        rows = pl.ds(part * hrows, hrows)
        return own[z_at(d) * CORES + core, rows, :] + cross[at_cross(d), rows, :]

    def arrived(way, dist, part):
        return ring_in[2 * dist - 2 + way, part * hrows : (part + 1) * hrows, :]

    def ring_step(dist, part):
        adds = dist != FAR and dist != JUMP_SUM - 1
        if adds:
            ring_wait(dist + 1, part)
        for way in (0, 1):
            if dist == FAR and part % 2 != way:
                continue
            value = total(FAR if dist == FAR else SIGN[way] * dist, part)
            if adds and (dist + 1 < FAR or part % 2 == way):
                value = value + arrived(way, dist + 1, part)
            ring_out[2 * dist - 2 + way, part * hrows : (part + 1) * hrows, :] = value
            ring_start(way, dist, part)

    def finish(part):
        value = total(0, part)
        for dist in sorted({1, JUMP_SUM}):
            ring_wait(dist, part)
            for way in (0, 1):
                value = value + arrived(way, dist, part)
        out_ref[part * hrows : (part + 1) * hrows, :] = value.astype(jnp.bfloat16)

    cross_start(8)
    cross_start(4)
    cross_wait(8)
    ring_step(8, 0)
    ring_step(8, 3)
    cross_wait(4)
    cross_start(7)
    ring_step(4, 0)
    ring_step(8, 2)
    ring_step(8, 1)
    ring_step(4, 1)
    cross_start(3)
    ring_step(4, 3)
    cross_start(6)
    cross_start(2)
    cross_start(5)
    ring_step(4, 2)
    cross_wait(7)
    cross_wait(3)
    ring_step(7, 0)
    cross_start(1)
    ring_step(3, 0)
    cross_wait(6)
    ring_step(7, 3)
    ring_step(3, 1)
    cross_wait(5)
    ring_step(7, 1)
    ring_step(3, 3)
    ring_step(7, 2)
    ring_step(3, 2)
    cross_wait(2)
    cross_start(0)
    ring_step(6, 0)
    ring_step(2, 0)
    ring_step(6, 3)
    ring_step(6, 1)
    ring_step(2, 3)
    ring_step(6, 2)
    ring_step(2, 1)
    cross_wait(0)
    ring_step(5, 0)
    ring_step(2, 2)
    ring_step(5, 3)
    ring_step(5, 1)
    ring_step(5, 2)
    cross_wait(1)
    ring_step(1, 2)
    ring_step(1, 3)
    ring_step(1, 0)
    ring_step(1, 1)
    finish(3)
    finish(0)
    finish(1)
    finish(2)

    some = gath.at[pl.ds(0, NP - 1)]
    pltpu.make_async_copy(some, some, xy_send).wait()
    tiles_wait(z_send, KT * (2 * FAR - 1))
    tiles_wait(c_send, KT * 2 * FAR)
    blocks_wait(own, x_send, NZ)
    blocks_wait(ring_out, r_send, 2 * FAR - 1)


def per_device(amplitudes, integrals, cd_index, ab_index, owner_map):
    shard = integrals.reshape(SHARD, T)
    dma = pltpu.SemaphoreType.DMA
    return pl.pallas_call(
        kernel,
        out_shape=jax.ShapeDtypeStruct((T, T), jnp.bfloat16),
        in_specs=[
            pl.BlockSpec(memory_space=pltpu.HBM),
            pl.BlockSpec(memory_space=pltpu.HBM),
            pl.BlockSpec(memory_space=pltpu.VMEM),
            pl.BlockSpec(memory_space=pltpu.HBM),
            pl.BlockSpec(memory_space=pltpu.HBM),
        ],
        out_specs=pl.BlockSpec(memory_space=pltpu.VMEM),
        scratch_shapes=[
            pltpu.SMEM((16, WIDE), jnp.int32),
            pltpu.VMEM((CAP, NI, NI), jnp.int32),
            pltpu.VMEM((CAP, NI, NI), jnp.int32),
            pltpu.VMEM((16, WIDE), jnp.int32),
            dma((2,)),
            pltpu.VMEM((NP, SHARD, T), jnp.bfloat16),
            pltpu.VMEM((CORES * NZ * KT, T, T), jnp.bfloat16),
            pltpu.VMEM((2 * CORES * KT, T, T), jnp.bfloat16),
            pltpu.VMEM((TILES, T, T), jnp.float32),
            pltpu.VMEM((TILES, T, T), jnp.float32),
            pltpu.VMEM((RES, T, T), jnp.float32),
            pltpu.VMEM((NZ, T, T), jnp.float32),
            pltpu.VMEM((2 * FAR, T, T), jnp.float32),
            pltpu.VMEM((2 * FAR, T, T), jnp.float32),
            dma, dma,
            dma, dma((BATCHES, 7)),
            dma, dma((FAR, KT)),
            dma, dma((2,)),
            dma, dma((FAR + 1,)),
            dma, dma((FAR, PARTS)),
        ],
        compiler_params=pltpu.CompilerParams(
            collective_id=0, has_side_effects=True, vmem_limit_bytes=VMEM
        ),
        name="ladder",
    )(cd_index.transpose(2, 0, 1), ab_index.transpose(2, 0, 1), owner_map.reshape(1, RES), amplitudes, shard)


def solution(mesh):
    return jax.shard_map(
        per_device,
        mesh=mesh,
        in_specs=(P("pair", "intg"), P("intg", None, None, "pair", None), P(), P(), P()),
        out_specs=P("pair", "intg"),
        check_vma=False,
    )
```

```python
import jax
import jax.numpy as jnp
from jax import lax
from jax.experimental import pallas as pl
from jax.experimental.pallas import tpu as pltpu
from jax.sharding import PartitionSpec as P

MESH = pl.DeviceIdType.MESH
NX, NY, NZ = 4, 4, 16
CORES = 2
T = 128
KT = 3
CAP = 5
NI = NZ * CORES
TILES = NI * CAP
ROWS = 8
SHARD = TILES * ROWS
NP = NX * NY
RES = 32
FAR = NZ // 2
BATCHES = 2
BATCH_TILES = TILES // BATCHES
CHUNK = SHARD // BATCHES // 2
QUAD_TILES = BATCH_TILES // 2
PIECE = CHUNK // 2
QUAD = 4
SOON = 5
JUMP_SUM = 5
PARTS = 4
UNROLL = 2
VMEM = 60 * 1024 * 1024


def quad_of(z, batch, half):
    side = 2 * ((z % QUAD) // 2) - 1
    step = (0, side, -side, 2)[2 * batch + half]
    return (z // QUAD + step + QUAD) % QUAD


PERM, KEEP, LAST, USED, WHICH = 0, 1, 2, 3, 4
GROUPS = BATCHES * RES
WIDE = 256


def iota(shape, dim):
    return lax.broadcasted_iota(jnp.int32, shape, dim)


def inside(value, count):
    return jnp.minimum(jnp.maximum(value, 0), count - 1)


def place_table(table, cd, ab, owner, z, g):
    f32, bf16 = jnp.float32, jnp.bfloat16

    def dot(a, b, dims=((1,), (0,))):
        return lax.dot_general(a.astype(bf16), b.astype(bf16), (dims, ((), ())), preferred_element_type=f32)

    eye = iota((RES, RES), 0) == iota((RES, RES), 1)
    owners = jnp.sum(jnp.where(eye, owner[...].astype(f32), 0.0), axis=1, keepdims=True)
    quad = iota((1, NI), 1) // (QUAD * CORES)
    early = (quad == quad_of(z, 0, 0)) | (quad == quad_of(z, 0, 1))
    member = jnp.zeros((GROUPS, WIDE), f32)
    for s in range(CAP):
        hit = owners == ab[s, pl.ds(g, 1), :].astype(f32)
        both = jnp.concatenate([jnp.where(hit & early, 1.0, 0.0), jnp.where(hit & ~early, 1.0, 0.0)], axis=0)
        spread = jnp.where(iota((NI, WIDE), 1) == iota((NI, WIDE), 0) + s * NI, 1.0, 0.0)
        member = member + dot(both, spread)
    before = dot(member, jnp.where(iota((WIDE, WIDE), 0) < iota((WIDE, WIDE), 1), 1.0, 0.0))
    counts = jnp.sum(member, axis=1, keepdims=True)
    lower = jnp.where(iota((GROUPS, GROUPS), 1) < iota((GROUPS, GROUPS), 0), 1.0, 0.0)
    starts = dot(lower, jnp.broadcast_to(counts, (GROUPS, T)))[:, :1]
    rank = jnp.sum(member * (starts + before), axis=0, keepdims=True).astype(jnp.int32)
    lane = iota((WIDE, WIDE), 1)
    moved = jnp.where((iota((WIDE, WIDE), 0) == rank) & (lane < TILES), 1.0, 0.0)
    tile = iota((8, WIDE), 1) % NI * CAP + iota((8, WIDE), 1) // NI
    perm = dot(tile, moved, ((1,), (1,)))
    full = counts > 0.0
    first = (iota((GROUPS, WIDE), 1).astype(f32) == starts) & full
    same = iota((GROUPS, WIDE), 1) == iota((GROUPS, WIDE), 0)
    last = jnp.where(same, jnp.clip(starts + counts - 1.0, 0.0, TILES - 1.0), 0.0)
    top = TILES - 1.0
    table[PERM : PERM + 1, :] = jnp.minimum(perm[:1], top).astype(jnp.int32)
    table[KEEP : KEEP + 1, :] = 1 - jnp.max(jnp.where(first, 1.0, 0.0), axis=0, keepdims=True).astype(jnp.int32)
    table[LAST : LAST + 1, :] = jnp.sum(last, axis=0, keepdims=True).astype(jnp.int32)
    table[USED : USED + 1, :] = jnp.max(jnp.where(same & full, 1.0, 0.0), axis=0, keepdims=True).astype(jnp.int32)
    for s in range(CAP):
        table[WHICH + s : WHICH + s + 1, :NI] = cd[s, pl.ds(g, 1), :]


def kernel(
    cd_hbm, ab_hbm, owner, amp_hbm, int_hbm, out_ref,
    table, cd, ab, table_vmem, index_sem,
    gath, amps, stage, prods, sums, own, cross, far_in, ring_in, ring_out,
    own_sem, amp_sem, xy_send, xy_recv, z_send, z_recv, c_send, c_recv,
    x_send, x_recv, r_send, r_recv,
):
    p = lax.axis_index("pair")
    g = lax.axis_index("intg")
    x, y = p // NY, p % NY
    z, core = g // CORES, g % CORES
    sib = 1 - core

    def flat(xy):
        return xy[0] * NY + xy[1]

    def xy_dev(xy):
        return (flat(xy), g)

    def z_at(d):
        return (z + d + 2 * NZ) % NZ

    def z_dev(d):
        return (p, z_at(d) * CORES + core)

    sib_dev = (p, z * CORES + sib)

    def remote(src, dst, ss, rs, to):
        return pltpu.make_async_remote_copy(
            src_ref=src, dst_ref=dst, send_sem=ss, recv_sem=rs, device_id=to, device_id_type=MESH
        )

    def place(h, da, db):
        ax, by = (da, db) if h == 0 else (db, da)
        return ((x + ax + NX) % NX, (y + by + NY) % NY)

    barrier = pltpu.get_barrier_semaphore()
    partners = [xy_dev(place(h, d, 0)) for h in (0, 1) for d in (1, -1)] + [sib_dev]
    partners += [z_dev(1), z_dev(-1)]
    for to in partners:
        pl.semaphore_signal(barrier, inc=1, device_id=to, device_id_type=MESH)

    own_copy = pltpu.make_async_copy(int_hbm, gath.at[p], own_sem)
    own_copy.start()
    own_amps = amps.at[pl.ds(core * (NZ * KT) + z * KT, KT)]
    for q in range(KT):
        pltpu.make_async_copy(amp_hbm.at[:, pl.ds(q * T, T)], own_amps.at[q], amp_sem).start()
    index_copies = [
        pltpu.make_async_copy(cd_hbm, cd, index_sem.at[0]), pltpu.make_async_copy(ab_hbm, ab, index_sem.at[1])
    ]
    for c in index_copies:
        c.start()
    pl.semaphore_wait(barrier, len(partners))

    SHIFT = (0, -1, 1, 2)
    FIRST, FIRST_FAR, SECOND, SECOND_FAR = 0, 1, 2, 6

    def xy_start(b, h, sem, who, to, part=None, own=False):
        start, count = pl.multiple_of(quad_of(z, b, h) * CHUNK, CHUNK), CHUNK
        if part is not None:
            start, count = start + part * PIECE, PIECE
        src = int_hbm if own else gath.at[flat(who)]
        remote(
            src.at[pl.ds(start, count)], gath.at[flat(who), pl.ds(start, count)],
            xy_send, xy_recv.at[b, sem], xy_dev(to),
        ).start()

    def xy_wait(b, sem, chunks):
        if chunks * CHUNK > SHARD:
            some = gath.at[pl.ds(0, chunks * CHUNK // SHARD)]
        else:
            some = gath.at[0, pl.ds(0, chunks * CHUNK)]
        pltpu.make_async_copy(some, some, xy_recv.at[b, sem]).wait()

    def first_own(b):
        for h in (0, 1):
            for d in (1, -1):
                xy_start(b, h, FIRST, place(h, 0, 0), place(h, d, 0), own=True)

    def second(b, q, own=False):
        for h in (0, 1):
            for d in (1, -1):
                xy_start(b, h, SECOND + q, place(h, SHIFT[q], 0), place(h, 0, d), own=own)

    def first_forward(b):
        xy_wait(b, FIRST, 4)
        for h in (0, 1):
            for d in (1, -1):
                xy_start(b, h, FIRST_FAR, place(h, -d, 0), place(h, d, 0), part=(1 - d) // 2)

    def first_far(b):
        xy_wait(b, FIRST_FAR, 2)
        second(b, 3)

    def second_forward(b, q):
        xy_wait(b, SECOND + q, 4)
        for h in (0, 1):
            for d in (1, -1):
                xy_start(b, h, SECOND_FAR, place(h, SHIFT[q], -d), place(h, 0, d), part=(1 - d) // 2)

    def second_far(b):
        xy_wait(b, SECOND_FAR, 8)

    SIGN = (1, -1)

    def tiles_wait(sem, count):
        some = amps.at[pl.ds(0, count)]
        pltpu.make_async_copy(some, some, sem).wait()

    def shard(owner_core, d):
        return amps.at[pl.ds(owner_core * (NZ * KT) + z_at(d) * KT, KT)]

    def z_start(dist, q):
        for way in (0, 1):
            part = shard(core, -SIGN[way] * (dist - 1)).at[q]
            if dist == FAR:
                part = part.at[pl.ds(way * (T // 2), T // 2)]
            remote(part, part, z_send, z_recv.at[dist - 1, q], z_dev(SIGN[way])).start()

    def to_sibling(dist):
        for way in (0,) if dist in (0, FAR) else (0, 1):
            part = shard(core, SIGN[way] * dist)
            remote(part, part, c_send, c_recv.at[0 if dist <= SOON else 1 if dist < FAR else 2], sib_dev).start()

    def from_sibling(n):
        tiles_wait(c_recv.at[n], KT * (1 + 2 * SOON, 2 * (FAR - 1 - SOON), 1)[n])

    def z_take(dist, q):
        tiles_wait(z_recv.at[dist - 1, q], 1 if dist == FAR else 2)
        if dist < FAR:
            z_start(dist + 1, q)
        if q == KT - 1:
            to_sibling(dist)

    def products(b, first, count):
        def body(n, carry):
            at = jnp.where(n < QUAD, quad_of(z, b, 0), quad_of(z, b, 1)) * QUAD + n % QUAD
            slot = n % 2 * (CORES * KT)
            for c in range(CORES):
                stage[pl.ds(slot + c * KT, KT)] = amps[pl.ds(c * (NZ * KT) + at * KT, KT)]
            for k in range(CAP):
                rows = pl.ds(pl.multiple_of(at * (2 * CAP * ROWS) + k * 2 * ROWS, 2 * ROWS), 2 * ROWS)
                group = gath[:, rows, :].astype(jnp.float32)
                for odd in (0, 1):
                    tile = group[:, odd * ROWS : (odd + 1) * ROWS, :].reshape(T, T).astype(jnp.bfloat16)
                    m = 2 * k + odd
                    which = inside(table[WHICH + m % CAP, at * CORES + m // CAP], KT)
                    prods[at * (2 * CAP) + m] = jnp.dot(
                        stage[slot + m // CAP * KT + which], tile, preferred_element_type=jnp.float32
                    )
            return carry

        lax.fori_loop(first, first + count, body, 0)

    def running(b):
        def body(t, acc):
            acc = jnp.where(table[KEEP, t] > 0, acc, 0.0) + prods[inside(table[PERM, t], TILES)]
            sums[t] = acc
            return acc

        lax.fori_loop(b * BATCH_TILES, (b + 1) * BATCH_TILES, body, jnp.zeros((T, T), jnp.float32))

    def slot_sum(b, r):
        at = b * RES + r
        return jnp.where(table[USED, at] > 0, sums[inside(table[LAST, at], TILES)], 0.0)

    def pick(b):
        def body(r, carry):
            value = slot_sum(b, r)
            own[r] = value if b == 0 else own[r] + value
            return carry

        lax.fori_loop(0, RES, body, 0)

    to_scalars = pltpu.make_async_copy(table_vmem, table, index_sem.at[0])

    def make_table():
        for c in index_copies:
            c.wait()
        place_table(table_vmem, cd, ab, owner, z, g)
        to_scalars.start()

    def table_done():
        to_scalars.wait()

    first_own(1)
    tiles_wait(amp_sem, KT)
    z_start(1, 0)
    first_own(0)
    z_start(1, 1)
    make_table()
    z_start(1, 2)
    second(1, 0, True)
    z_take(1, 0)
    second(0, 0, True)
    z_take(1, 1)
    z_take(1, 2)
    first_forward(0)
    second(0, 1)
    z_take(2, 0)
    first_forward(1)
    z_take(2, 1)
    second(0, 2)
    second(1, 1)
    z_take(2, 2)
    z_take(3, 0)
    first_far(0)
    z_take(3, 1)
    z_take(3, 2)
    second(1, 2)
    z_take(4, 0)
    first_far(1)
    z_take(4, 1)
    z_take(4, 2)
    z_take(5, 0)
    second_forward(0, 1)
    second_forward(0, 2)
    z_take(5, 1)
    second_forward(0, 0)
    z_take(5, 2)
    second_forward(0, 3)
    to_sibling(0)
    z_take(6, 0)
    second_forward(1, 3)
    second_forward(1, 0)
    from_sibling(0)
    z_take(6, 1)
    second_forward(1, 2)
    second_forward(1, 1)
    z_take(6, 2)
    second_far(0)
    own_copy.wait()
    table_done()
    products(0, 0, 2)
    z_take(7, 0)
    products(0, 4, 2)
    z_take(7, 1)
    products(0, 2, 2)
    z_take(7, 2)
    products(0, 6, 2)
    running(0)
    pick(0)
    second_far(1)
    z_take(8, 0)
    from_sibling(1)
    z_take(8, 1)
    z_take(8, 2)
    products(1, 0, 4)
    from_sibling(2)
    products(1, 4, 4)
    running(1)
    pick(1)

    def both(dist):
        return (0,) if dist == 0 else (dist, -dist)

    def blocks_wait(ref, sem, count):
        some = ref.at[pl.ds(0, count)]
        pltpu.make_async_copy(some, some, sem).wait()

    def cross_start(dist):
        for d in both(dist):
            remote(own.at[z_at(d) * CORES + sib], cross.at[FAR - 1 + d], x_send, x_recv.at[dist], sib_dev).start()

    def cross_wait(dist):
        blocks_wait(cross, x_recv.at[dist], len(both(dist)))

    hrows = T // PARTS

    def ring_start(way, dist, part):
        rows = pl.ds(part * hrows, hrows)
        hop = JUMP_SUM if dist == JUMP_SUM else 1
        remote(
            ring_out.at[2 * dist - 2 + way, rows], ring_in.at[2 * dist - 2 + way, rows],
            r_send, r_recv.at[dist - 1, part], z_dev(SIGN[way] * hop),
        ).start()

    def far_start(part):
        way = part % 2
        rows = pl.ds(part * hrows, hrows)
        to = z_at(SIGN[way]) * CORES
        block = z_at(FAR) * CORES
        remote(
            own.at[block + core, rows], ring_in.at[2 * FAR - 2 + way, rows],
            r_send, r_recv.at[FAR - 1, part], (p, to + core),
        ).start()
        remote(
            own.at[block + sib, rows], far_in.at[way, rows],
            r_send, r_recv.at[FAR - 1, part], (p, to + sib),
        ).start()

    def ring_wait(dist, part):
        some = ring_in.at[0, pl.ds(0, 2 * hrows)]
        pltpu.make_async_copy(some, some, r_recv.at[dist - 1, part]).wait()

    def total(d, part):
        rows = pl.ds(part * hrows, hrows)
        return own[z_at(d) * CORES + core, rows, :] + cross[FAR - 1 + d, rows, :]

    def arrived(way, dist, part):
        return ring_in[2 * dist - 2 + way, part * hrows : (part + 1) * hrows, :]

    def ring_step(dist, part):
        adds = dist != JUMP_SUM - 1
        if adds:
            ring_wait(dist + 1, part)
        for way in (0, 1):
            value = total(SIGN[way] * dist, part)
            if adds and (dist + 1 < FAR or part % 2 == way):
                value = value + arrived(way, dist + 1, part)
            if dist + 1 == FAR and part % 2 == way:
                value = value + far_in[way, part * hrows : (part + 1) * hrows, :]
            ring_out[2 * dist - 2 + way, part * hrows : (part + 1) * hrows, :] = value
            ring_start(way, dist, part)

    def finish(part):
        value = total(0, part)
        for dist in sorted({1, JUMP_SUM}):
            ring_wait(dist, part)
            for way in (0, 1):
                value = value + arrived(way, dist, part)
        out_ref[part * hrows : (part + 1) * hrows, :] = value.astype(jnp.bfloat16)

    far_start(0)
    far_start(1)
    far_start(2)
    far_start(3)
    cross_start(4)
    cross_start(7)
    cross_wait(4)
    ring_step(4, 0)
    ring_step(4, 1)
    cross_start(3)
    ring_step(4, 3)
    cross_start(6)
    cross_start(2)
    cross_start(5)
    ring_step(4, 2)
    cross_wait(7)
    cross_wait(3)
    ring_step(7, 0)
    cross_start(1)
    ring_step(3, 0)
    cross_wait(6)
    ring_step(7, 3)
    ring_step(3, 1)
    cross_wait(5)
    ring_step(7, 1)
    ring_step(3, 3)
    ring_step(7, 2)
    ring_step(3, 2)
    cross_wait(2)
    cross_start(0)
    ring_step(6, 0)
    ring_step(2, 0)
    ring_step(6, 3)
    ring_step(6, 1)
    ring_step(2, 3)
    ring_step(6, 2)
    ring_step(2, 1)
    cross_wait(0)
    ring_step(5, 0)
    ring_step(2, 2)
    ring_step(5, 3)
    ring_step(5, 1)
    ring_step(5, 2)
    cross_wait(1)
    ring_step(1, 2)
    ring_step(1, 3)
    ring_step(1, 0)
    ring_step(1, 1)
    finish(3)
    finish(0)
    finish(1)
    finish(2)

    some = gath.at[pl.ds(0, NP - 1)]
    pltpu.make_async_copy(some, some, xy_send).wait()
    tiles_wait(z_send, KT * (2 * FAR - 1))
    tiles_wait(c_send, KT * 2 * FAR)
    blocks_wait(own, x_send, NZ - 1)
    blocks_wait(ring_out, r_send, 2 * FAR)


def per_device(amplitudes, integrals, cd_index, ab_index, owner_map):
    shard = integrals.reshape(SHARD, T)
    dma = pltpu.SemaphoreType.DMA
    return pl.pallas_call(
        kernel,
        out_shape=jax.ShapeDtypeStruct((T, T), jnp.bfloat16),
        in_specs=[
            pl.BlockSpec(memory_space=pltpu.HBM),
            pl.BlockSpec(memory_space=pltpu.HBM),
            pl.BlockSpec(memory_space=pltpu.VMEM),
            pl.BlockSpec(memory_space=pltpu.HBM),
            pl.BlockSpec(memory_space=pltpu.HBM),
        ],
        out_specs=pl.BlockSpec(memory_space=pltpu.VMEM),
        scratch_shapes=[
            pltpu.SMEM((16, WIDE), jnp.int32),
            pltpu.VMEM((CAP, NI, NI), jnp.int32),
            pltpu.VMEM((CAP, NI, NI), jnp.int32),
            pltpu.VMEM((16, WIDE), jnp.int32),
            dma((2,)),
            pltpu.VMEM((NP, SHARD, T), jnp.bfloat16),
            pltpu.VMEM((CORES * NZ * KT, T, T), jnp.bfloat16),
            pltpu.VMEM((2 * CORES * KT, T, T), jnp.bfloat16),
            pltpu.VMEM((TILES, T, T), jnp.float32),
            pltpu.VMEM((TILES, T, T), jnp.float32),
            pltpu.VMEM((RES, T, T), jnp.float32),
            pltpu.VMEM((NZ - 1, T, T), jnp.float32),
            pltpu.VMEM((2, T, T), jnp.float32),
            pltpu.VMEM((2 * FAR, T, T), jnp.float32),
            pltpu.VMEM((2 * FAR, T, T), jnp.float32),
            dma, dma,
            dma, dma((BATCHES, 7)),
            dma, dma((FAR, KT)),
            dma, dma((3,)),
            dma, dma((FAR,)),
            dma, dma((FAR, PARTS)),
        ],
        compiler_params=pltpu.CompilerParams(
            collective_id=0, has_side_effects=True, vmem_limit_bytes=VMEM
        ),
        name="ladder",
    )(cd_index.transpose(2, 0, 1), ab_index.transpose(2, 0, 1), owner_map.reshape(1, RES), amplitudes, shard)


def solution(mesh):
    return jax.shard_map(
        per_device,
        mesh=mesh,
        in_specs=(P("pair", "intg"), P("intg", None, None, "pair", None), P(), P(), P()),
        out_specs=P("pair", "intg"),
        check_vma=False,
    )
```

```python
import jax
import jax.numpy as jnp
from jax import lax
from jax.experimental import pallas as pl
from jax.experimental.pallas import tpu as pltpu
from jax.sharding import PartitionSpec as P

MESH = pl.DeviceIdType.MESH
NX, NY, NZ = 4, 4, 16
CORES = 2
T = 128
KT = 3
CAP = 5
NI = NZ * CORES
TILES = NI * CAP
ROWS = 8
SHARD = TILES * ROWS
NP = NX * NY
RES = 32
FAR = NZ // 2
BATCHES = 2
BATCH_TILES = TILES // BATCHES
CHUNK = SHARD // BATCHES // 2
QUAD_TILES = BATCH_TILES // 2
PIECE = CHUNK // 2
QUAD = 4
SOON = 5
JUMP_SUM = 5
PARTS = 4
UNROLL = 2
VMEM = 60 * 1024 * 1024


def quad_of(z, batch, half):
    side = 2 * ((z % QUAD) // 2) - 1
    step = (0, side, -side, 2)[2 * batch + half]
    return (z // QUAD + step + QUAD) % QUAD


PERM, KEEP, LAST, USED, WHICH = 0, 1, 2, 3, 4
GROUPS = BATCHES * RES
WIDE = 256


def iota(shape, dim):
    return lax.broadcasted_iota(jnp.int32, shape, dim)


def inside(value, count):
    return jnp.minimum(jnp.maximum(value, 0), count - 1)


def place_table(table, cd, ab, owner, z, g):
    f32, bf16 = jnp.float32, jnp.bfloat16

    def dot(a, b, dims=((1,), (0,))):
        return lax.dot_general(a.astype(bf16), b.astype(bf16), (dims, ((), ())), preferred_element_type=f32)

    eye = iota((RES, RES), 0) == iota((RES, RES), 1)
    owners = jnp.sum(jnp.where(eye, owner[...].astype(f32), 0.0), axis=1, keepdims=True)
    quad = iota((1, NI), 1) // (QUAD * CORES)
    early = (quad == quad_of(z, 0, 0)) | (quad == quad_of(z, 0, 1))
    member = jnp.zeros((GROUPS, WIDE), f32)
    for s in range(CAP):
        hit = owners == ab[s, pl.ds(g, 1), :].astype(f32)
        both = jnp.concatenate([jnp.where(hit & early, 1.0, 0.0), jnp.where(hit & ~early, 1.0, 0.0)], axis=0)
        spread = jnp.where(iota((NI, WIDE), 1) == iota((NI, WIDE), 0) + s * NI, 1.0, 0.0)
        member = member + dot(both, spread)
    before = dot(member, jnp.where(iota((WIDE, WIDE), 0) < iota((WIDE, WIDE), 1), 1.0, 0.0))
    counts = jnp.sum(member, axis=1, keepdims=True)
    lower = jnp.where(iota((GROUPS, GROUPS), 1) < iota((GROUPS, GROUPS), 0), 1.0, 0.0)
    starts = dot(lower, jnp.broadcast_to(counts, (GROUPS, T)))[:, :1]
    rank = jnp.sum(member * (starts + before), axis=0, keepdims=True).astype(jnp.int32)
    lane = iota((WIDE, WIDE), 1)
    moved = jnp.where((iota((WIDE, WIDE), 0) == rank) & (lane < TILES), 1.0, 0.0)
    tile = iota((8, WIDE), 1) % NI * CAP + iota((8, WIDE), 1) // NI
    perm = dot(tile, moved, ((1,), (1,)))
    full = counts > 0.0
    first = (iota((GROUPS, WIDE), 1).astype(f32) == starts) & full
    same = iota((GROUPS, WIDE), 1) == iota((GROUPS, WIDE), 0)
    last = jnp.where(same, jnp.clip(starts + counts - 1.0, 0.0, TILES - 1.0), 0.0)
    top = TILES - 1.0
    table[PERM : PERM + 1, :] = jnp.minimum(perm[:1], top).astype(jnp.int32)
    table[KEEP : KEEP + 1, :] = 1 - jnp.max(jnp.where(first, 1.0, 0.0), axis=0, keepdims=True).astype(jnp.int32)
    table[LAST : LAST + 1, :] = jnp.sum(last, axis=0, keepdims=True).astype(jnp.int32)
    table[USED : USED + 1, :] = jnp.max(jnp.where(same & full, 1.0, 0.0), axis=0, keepdims=True).astype(jnp.int32)
    for s in range(CAP):
        table[WHICH + s : WHICH + s + 1, :NI] = cd[s, pl.ds(g, 1), :]


def kernel(
    cd_hbm, ab_hbm, owner, amp_hbm, int_hbm, out_ref,
    table, cd, ab, table_vmem, index_sem,
    gath, amps, stage, prods, sums, own, cross, far_in, ring_in, ring_out,
    own_sem, amp_sem, xy_send, xy_recv, z_send, z_recv, c_send, c_recv,
    x_send, x_recv, r_send, r_recv,
):
    p = lax.axis_index("pair")
    g = lax.axis_index("intg")
    x, y = p // NY, p % NY
    z, core = g // CORES, g % CORES
    sib = 1 - core

    def flat(xy):
        return xy[0] * NY + xy[1]

    def xy_dev(xy):
        return (flat(xy), g)

    def z_at(d):
        return (z + d + 2 * NZ) % NZ

    def z_dev(d):
        return (p, z_at(d) * CORES + core)

    sib_dev = (p, z * CORES + sib)

    def remote(src, dst, ss, rs, to):
        return pltpu.make_async_remote_copy(
            src_ref=src, dst_ref=dst, send_sem=ss, recv_sem=rs, device_id=to, device_id_type=MESH
        )

    def place(h, da, db):
        ax, by = (da, db) if h == 0 else (db, da)
        return ((x + ax + NX) % NX, (y + by + NY) % NY)

    barrier = pltpu.get_barrier_semaphore()
    partners = [xy_dev(place(h, d, 0)) for h in (0, 1) for d in (1, -1)] + [sib_dev]
    partners += [z_dev(1), z_dev(-1)]
    for to in partners:
        pl.semaphore_signal(barrier, inc=1, device_id=to, device_id_type=MESH)

    own_copy = pltpu.make_async_copy(int_hbm, gath.at[p], own_sem)
    own_copy.start()
    own_amps = amps.at[pl.ds(core * (NZ * KT) + z * KT, KT)]
    for q in range(KT):
        pltpu.make_async_copy(amp_hbm.at[:, pl.ds(q * T, T)], own_amps.at[q], amp_sem).start()
    index_copies = [
        pltpu.make_async_copy(cd_hbm, cd, index_sem.at[0]), pltpu.make_async_copy(ab_hbm, ab, index_sem.at[1])
    ]
    for c in index_copies:
        c.start()
    pl.semaphore_wait(barrier, len(partners))

    SHIFT = (0, -1, 1, 2)
    FIRST, FIRST_FAR, SECOND, SECOND_FAR = 0, 1, 2, 6

    def xy_start(b, h, sem, who, to, part=None, own=False):
        start, count = pl.multiple_of(quad_of(z, b, h) * CHUNK, CHUNK), CHUNK
        if part is not None:
            start, count = start + part * PIECE, PIECE
        src = int_hbm if own else gath.at[flat(who)]
        remote(
            src.at[pl.ds(start, count)], gath.at[flat(who), pl.ds(start, count)],
            xy_send, xy_recv.at[b, sem], xy_dev(to),
        ).start()

    def xy_wait(b, sem, chunks):
        if chunks * CHUNK > SHARD:
            some = gath.at[pl.ds(0, chunks * CHUNK // SHARD)]
        else:
            some = gath.at[0, pl.ds(0, chunks * CHUNK)]
        pltpu.make_async_copy(some, some, xy_recv.at[b, sem]).wait()

    def first_own(b):
        for h in (0, 1):
            for d in (1, -1):
                xy_start(b, h, FIRST, place(h, 0, 0), place(h, d, 0), own=True)

    def second(b, q, own=False):
        for h in (0, 1):
            for d in (1, -1):
                xy_start(b, h, SECOND + q, place(h, SHIFT[q], 0), place(h, 0, d), own=own)

    def first_forward(b):
        xy_wait(b, FIRST, 4)
        for h in (0, 1):
            for d in (1, -1):
                xy_start(b, h, FIRST_FAR, place(h, -d, 0), place(h, d, 0), part=(1 - d) // 2)

    def first_far(b):
        xy_wait(b, FIRST_FAR, 2)
        second(b, 3)

    def second_forward(b, q):
        xy_wait(b, SECOND + q, 4)
        for h in (0, 1):
            for d in (1, -1):
                xy_start(b, h, SECOND_FAR, place(h, SHIFT[q], -d), place(h, 0, d), part=(1 - d) // 2)

    def second_far(b):
        xy_wait(b, SECOND_FAR, 8)

    SIGN = (1, -1)

    def tiles_wait(sem, count):
        some = amps.at[pl.ds(0, count)]
        pltpu.make_async_copy(some, some, sem).wait()

    def shard(owner_core, d):
        return amps.at[pl.ds(owner_core * (NZ * KT) + z_at(d) * KT, KT)]

    def z_start(dist, q):
        for way in (0, 1):
            part = shard(core, -SIGN[way] * (dist - 1)).at[q]
            if dist == FAR:
                part = part.at[pl.ds(way * (T // 2), T // 2)]
            remote(part, part, z_send, z_recv.at[dist - 1, q], z_dev(SIGN[way])).start()

    def to_sibling(dist):
        for way in (0,) if dist in (0, FAR) else (0, 1):
            part = shard(core, SIGN[way] * dist)
            remote(part, part, c_send, c_recv.at[0 if dist <= SOON else 1 if dist < FAR else 2], sib_dev).start()

    def from_sibling(n):
        tiles_wait(c_recv.at[n], KT * (1 + 2 * SOON, 2 * (FAR - 1 - SOON), 1)[n])

    def z_take(dist, q):
        tiles_wait(z_recv.at[dist - 1, q], 1 if dist == FAR else 2)
        if dist < FAR:
            z_start(dist + 1, q)
        if q == KT - 1:
            to_sibling(dist)

    def products(b, first, count):
        def body(n, carry):
            at = jnp.where(n < QUAD, quad_of(z, b, 0), quad_of(z, b, 1)) * QUAD + n % QUAD
            slot = n % 2 * (CORES * KT)
            for c in range(CORES):
                stage[pl.ds(slot + c * KT, KT)] = amps[pl.ds(c * (NZ * KT) + at * KT, KT)]
            for k in range(CAP):
                rows = pl.ds(pl.multiple_of(at * (2 * CAP * ROWS) + k * 2 * ROWS, 2 * ROWS), 2 * ROWS)
                group = gath[:, rows, :].astype(jnp.float32)
                for odd in (0, 1):
                    tile = group[:, odd * ROWS : (odd + 1) * ROWS, :].reshape(T, T).astype(jnp.bfloat16)
                    m = 2 * k + odd
                    which = inside(table[WHICH + m % CAP, at * CORES + m // CAP], KT)
                    prods[at * (2 * CAP) + m] = jnp.dot(
                        stage[slot + m // CAP * KT + which], tile, preferred_element_type=jnp.float32
                    )
            return carry

        lax.fori_loop(first, first + count, body, 0, unroll=2)

    def running(b):
        def body(t, acc):
            acc = jnp.where(table[KEEP, t] > 0, acc, 0.0) + prods[inside(table[PERM, t], TILES)]
            sums[t] = acc
            return acc

        lax.fori_loop(b * BATCH_TILES, (b + 1) * BATCH_TILES, body, jnp.zeros((T, T), jnp.float32), unroll=8)

    def slot_sum(b, r):
        at = b * RES + r
        return jnp.where(table[USED, at] > 0, sums[inside(table[LAST, at], TILES)], 0.0)

    def pick(b):
        def body(r, carry):
            value = slot_sum(b, r)
            own[r] = value if b == 0 else own[r] + value
            return carry

        lax.fori_loop(0, RES, body, 0, unroll=8)

    to_scalars = pltpu.make_async_copy(table_vmem, table, index_sem.at[0])

    def make_table():
        for c in index_copies:
            c.wait()
        place_table(table_vmem, cd, ab, owner, z, g)
        to_scalars.start()

    def table_done():
        to_scalars.wait()

    first_own(1)
    tiles_wait(amp_sem, KT)
    z_start(1, 0)
    first_own(0)
    z_start(1, 1)
    make_table()
    z_start(1, 2)
    second(1, 0, True)
    z_take(1, 0)
    second(0, 0, True)
    z_take(1, 1)
    z_take(1, 2)
    first_forward(0)
    second(0, 1)
    z_take(2, 0)
    first_forward(1)
    z_take(2, 1)
    second(0, 2)
    second(1, 1)
    z_take(2, 2)
    z_take(3, 0)
    first_far(0)
    z_take(3, 1)
    z_take(3, 2)
    second(1, 2)
    z_take(4, 0)
    first_far(1)
    z_take(4, 1)
    z_take(4, 2)
    z_take(5, 0)
    second_forward(0, 1)
    second_forward(0, 2)
    z_take(5, 1)
    second_forward(0, 0)
    z_take(5, 2)
    second_forward(0, 3)
    to_sibling(0)
    z_take(6, 0)
    second_forward(1, 3)
    second_forward(1, 0)
    from_sibling(0)
    z_take(6, 1)
    second_forward(1, 2)
    second_forward(1, 1)
    z_take(6, 2)
    second_far(0)
    own_copy.wait()
    table_done()
    products(0, 0, 2)
    z_take(7, 0)
    products(0, 4, 2)
    z_take(7, 1)
    products(0, 2, 2)
    z_take(7, 2)
    products(0, 6, 2)
    running(0)
    pick(0)
    second_far(1)
    z_take(8, 0)
    from_sibling(1)
    z_take(8, 1)
    z_take(8, 2)
    products(1, 0, 4)
    from_sibling(2)
    products(1, 4, 4)
    running(1)
    pick(1)

    def both(dist):
        return (0,) if dist == 0 else (dist, -dist)

    def blocks_wait(ref, sem, count):
        some = ref.at[pl.ds(0, count)]
        pltpu.make_async_copy(some, some, sem).wait()

    def cross_start(dist):
        for d in both(dist):
            remote(own.at[z_at(d) * CORES + sib], cross.at[FAR - 1 + d], x_send, x_recv.at[dist], sib_dev).start()

    def cross_wait(dist):
        blocks_wait(cross, x_recv.at[dist], len(both(dist)))

    hrows = T // PARTS

    def ring_start(way, dist, part):
        rows = pl.ds(part * hrows, hrows)
        hop = JUMP_SUM if dist == JUMP_SUM else 1
        remote(
            ring_out.at[2 * dist - 2 + way, rows], ring_in.at[2 * dist - 2 + way, rows],
            r_send, r_recv.at[dist - 1, part], z_dev(SIGN[way] * hop),
        ).start()

    def far_start(part):
        way = part % 2
        rows = pl.ds(part * hrows, hrows)
        to = z_at(SIGN[way]) * CORES
        block = z_at(FAR) * CORES
        remote(
            own.at[block + core, rows], ring_in.at[2 * FAR - 2 + way, rows],
            r_send, r_recv.at[FAR - 1, part], (p, to + core),
        ).start()
        remote(
            own.at[block + sib, rows], far_in.at[way, rows],
            r_send, r_recv.at[FAR - 1, part], (p, to + sib),
        ).start()

    def ring_wait(dist, part):
        some = ring_in.at[0, pl.ds(0, 2 * hrows)]
        pltpu.make_async_copy(some, some, r_recv.at[dist - 1, part]).wait()

    def total(d, part):
        rows = pl.ds(part * hrows, hrows)
        return own[z_at(d) * CORES + core, rows, :] + cross[FAR - 1 + d, rows, :]

    def arrived(way, dist, part):
        return ring_in[2 * dist - 2 + way, part * hrows : (part + 1) * hrows, :]

    def ring_step(dist, part):
        adds = dist != JUMP_SUM - 1
        if adds:
            ring_wait(dist + 1, part)
        for way in (0, 1):
            value = total(SIGN[way] * dist, part)
            if adds and (dist + 1 < FAR or part % 2 == way):
                value = value + arrived(way, dist + 1, part)
            if dist + 1 == FAR and part % 2 == way:
                value = value + far_in[way, part * hrows : (part + 1) * hrows, :]
            ring_out[2 * dist - 2 + way, part * hrows : (part + 1) * hrows, :] = value
            ring_start(way, dist, part)

    def finish(part):
        value = total(0, part)
        for dist in sorted({1, JUMP_SUM}):
            ring_wait(dist, part)
            for way in (0, 1):
                value = value + arrived(way, dist, part)
        out_ref[part * hrows : (part + 1) * hrows, :] = value.astype(jnp.bfloat16)

    far_start(0)
    far_start(1)
    far_start(2)
    far_start(3)
    cross_start(4)
    cross_start(7)
    cross_wait(4)
    ring_step(4, 0)
    ring_step(4, 1)
    cross_start(3)
    ring_step(4, 3)
    cross_start(6)
    cross_start(2)
    cross_start(5)
    ring_step(4, 2)
    cross_wait(7)
    cross_wait(3)
    ring_step(7, 0)
    cross_start(1)
    ring_step(3, 0)
    cross_wait(6)
    ring_step(7, 3)
    ring_step(3, 1)
    cross_wait(5)
    ring_step(7, 1)
    ring_step(3, 3)
    ring_step(7, 2)
    ring_step(3, 2)
    cross_wait(2)
    cross_start(0)
    ring_step(6, 0)
    ring_step(2, 0)
    ring_step(6, 3)
    ring_step(6, 1)
    ring_step(2, 3)
    ring_step(6, 2)
    ring_step(2, 1)
    cross_wait(0)
    ring_step(5, 0)
    ring_step(2, 2)
    ring_step(5, 3)
    ring_step(5, 1)
    ring_step(5, 2)
    cross_wait(1)
    ring_step(1, 2)
    ring_step(1, 3)
    ring_step(1, 0)
    ring_step(1, 1)
    finish(3)
    finish(0)
    finish(1)
    finish(2)

    some = gath.at[pl.ds(0, NP - 1)]
    pltpu.make_async_copy(some, some, xy_send).wait()
    tiles_wait(z_send, KT * (2 * FAR - 1))
    tiles_wait(c_send, KT * 2 * FAR)
    blocks_wait(own, x_send, NZ - 1)
    blocks_wait(ring_out, r_send, 2 * FAR)


def per_device(amplitudes, integrals, cd_index, ab_index, owner_map):
    shard = integrals.reshape(SHARD, T)
    dma = pltpu.SemaphoreType.DMA
    return pl.pallas_call(
        kernel,
        out_shape=jax.ShapeDtypeStruct((T, T), jnp.bfloat16),
        in_specs=[
            pl.BlockSpec(memory_space=pltpu.HBM),
            pl.BlockSpec(memory_space=pltpu.HBM),
            pl.BlockSpec(memory_space=pltpu.VMEM),
            pl.BlockSpec(memory_space=pltpu.HBM),
            pl.BlockSpec(memory_space=pltpu.HBM),
        ],
        out_specs=pl.BlockSpec(memory_space=pltpu.VMEM),
        scratch_shapes=[
            pltpu.SMEM((16, WIDE), jnp.int32),
            pltpu.VMEM((CAP, NI, NI), jnp.int32),
            pltpu.VMEM((CAP, NI, NI), jnp.int32),
            pltpu.VMEM((16, WIDE), jnp.int32),
            dma((2,)),
            pltpu.VMEM((NP, SHARD, T), jnp.bfloat16),
            pltpu.VMEM((CORES * NZ * KT, T, T), jnp.bfloat16),
            pltpu.VMEM((2 * CORES * KT, T, T), jnp.bfloat16),
            pltpu.VMEM((TILES, T, T), jnp.float32),
            pltpu.VMEM((TILES, T, T), jnp.float32),
            pltpu.VMEM((RES, T, T), jnp.float32),
            pltpu.VMEM((NZ - 1, T, T), jnp.float32),
            pltpu.VMEM((2, T, T), jnp.float32),
            pltpu.VMEM((2 * FAR, T, T), jnp.float32),
            pltpu.VMEM((2 * FAR, T, T), jnp.float32),
            dma, dma,
            dma, dma((BATCHES, 7)),
            dma, dma((FAR, KT)),
            dma, dma((3,)),
            dma, dma((FAR,)),
            dma, dma((FAR, PARTS)),
        ],
        compiler_params=pltpu.CompilerParams(
            collective_id=0, has_side_effects=True, vmem_limit_bytes=VMEM
        ),
        name="ladder",
    )(cd_index.transpose(2, 0, 1), ab_index.transpose(2, 0, 1), owner_map.reshape(1, RES), amplitudes, shard)


def solution(mesh):
    return jax.shard_map(
        per_device,
        mesh=mesh,
        in_specs=(P("pair", "intg"), P("intg", None, None, "pair", None), P(), P(), P()),
        out_specs=P("pair", "intg"),
        check_vma=False,
    )
```

```python
import jax
import jax.numpy as jnp
from jax import lax
from jax.experimental import pallas as pl
from jax.experimental.pallas import tpu as pltpu
from jax.sharding import PartitionSpec as P

MESH = pl.DeviceIdType.MESH
NX, NY, NZ = 4, 4, 16
CORES = 2
T = 128
KT = 3
CAP = 5
NI = NZ * CORES
TILES = NI * CAP
ROWS = 8
SHARD = TILES * ROWS
NP = NX * NY
RES = 32
FAR = NZ // 2
BATCHES = 2
BATCH_TILES = TILES // BATCHES
CHUNK = SHARD // BATCHES // 2
QUAD_TILES = BATCH_TILES // 2
PIECE = CHUNK // 2
QUAD = 4
SOON = 5
JUMP_SUM = 5
PARTS = 4
UNROLL = 2
VMEM = 60 * 1024 * 1024


def quad_of(z, batch, half):
    side = 2 * ((z % QUAD) // 2) - 1
    step = (0, side, -side, 2)[2 * batch + half]
    return (z // QUAD + step + QUAD) % QUAD


PERM, KEEP, LAST, USED, WHICH = 0, 1, 2, 3, 4
GROUPS = BATCHES * RES
WIDE = 256


def iota(shape, dim):
    return lax.broadcasted_iota(jnp.int32, shape, dim)


def inside(value, count):
    return jnp.minimum(jnp.maximum(value, 0), count - 1)


def place_table(table, cd, ab, owner, z, g):
    f32, bf16 = jnp.float32, jnp.bfloat16

    def dot(a, b, dims=((1,), (0,))):
        return lax.dot_general(a.astype(bf16), b.astype(bf16), (dims, ((), ())), preferred_element_type=f32)

    eye = iota((RES, RES), 0) == iota((RES, RES), 1)
    owners = jnp.sum(jnp.where(eye, owner[...].astype(f32), 0.0), axis=1, keepdims=True)
    quad = iota((1, NI), 1) // (QUAD * CORES)
    early = (quad == quad_of(z, 0, 0)) | (quad == quad_of(z, 0, 1))
    member = jnp.zeros((GROUPS, WIDE), f32)
    for s in range(CAP):
        hit = owners == ab[s, pl.ds(g, 1), :].astype(f32)
        both = jnp.concatenate([jnp.where(hit & early, 1.0, 0.0), jnp.where(hit & ~early, 1.0, 0.0)], axis=0)
        spread = jnp.where(iota((NI, WIDE), 1) == iota((NI, WIDE), 0) + s * NI, 1.0, 0.0)
        member = member + dot(both, spread)
    before = dot(member, jnp.where(iota((WIDE, WIDE), 0) < iota((WIDE, WIDE), 1), 1.0, 0.0))
    counts = jnp.sum(member, axis=1, keepdims=True)
    lower = jnp.where(iota((GROUPS, GROUPS), 1) < iota((GROUPS, GROUPS), 0), 1.0, 0.0)
    starts = dot(lower, jnp.broadcast_to(counts, (GROUPS, T)))[:, :1]
    rank = jnp.sum(member * (starts + before), axis=0, keepdims=True).astype(jnp.int32)
    lane = iota((WIDE, WIDE), 1)
    moved = jnp.where((iota((WIDE, WIDE), 0) == rank) & (lane < TILES), 1.0, 0.0)
    tile = iota((8, WIDE), 1) % NI * CAP + iota((8, WIDE), 1) // NI
    perm = dot(tile, moved, ((1,), (1,)))
    full = counts > 0.0
    first = (iota((GROUPS, WIDE), 1).astype(f32) == starts) & full
    same = iota((GROUPS, WIDE), 1) == iota((GROUPS, WIDE), 0)
    last = jnp.where(same, jnp.clip(starts + counts - 1.0, 0.0, TILES - 1.0), 0.0)
    top = TILES - 1.0
    table[PERM : PERM + 1, :] = jnp.minimum(perm[:1], top).astype(jnp.int32)
    table[KEEP : KEEP + 1, :] = 1 - jnp.max(jnp.where(first, 1.0, 0.0), axis=0, keepdims=True).astype(jnp.int32)
    table[LAST : LAST + 1, :] = jnp.sum(last, axis=0, keepdims=True).astype(jnp.int32)
    table[USED : USED + 1, :] = jnp.max(jnp.where(same & full, 1.0, 0.0), axis=0, keepdims=True).astype(jnp.int32)
    for s in range(CAP):
        table[WHICH + s : WHICH + s + 1, :NI] = cd[s, pl.ds(g, 1), :]


def kernel(
    cd_hbm, ab_hbm, owner, amp_hbm, int_hbm, out_ref,
    table, cd, ab, table_vmem, index_sem,
    gath, amps, stage, prods, sums, own, cross, far_in, ring_in, ring_out,
    own_sem, amp_sem, xy_send, xy_recv, z_send, z_recv, c_send, c_recv,
    x_send, x_recv, r_send, r_recv,
):
    p = lax.axis_index("pair")
    g = lax.axis_index("intg")
    x, y = p // NY, p % NY
    z, core = g // CORES, g % CORES
    sib = 1 - core

    def flat(xy):
        return xy[0] * NY + xy[1]

    def xy_dev(xy):
        return (flat(xy), g)

    def z_at(d):
        return (z + d + 2 * NZ) % NZ

    def z_dev(d):
        return (p, z_at(d) * CORES + core)

    sib_dev = (p, z * CORES + sib)

    def remote(src, dst, ss, rs, to):
        return pltpu.make_async_remote_copy(
            src_ref=src, dst_ref=dst, send_sem=ss, recv_sem=rs, device_id=to, device_id_type=MESH
        )

    def place(h, da, db):
        ax, by = (da, db) if h == 0 else (db, da)
        return ((x + ax + NX) % NX, (y + by + NY) % NY)

    barrier = pltpu.get_barrier_semaphore()
    partners = [xy_dev(place(h, d, 0)) for h in (0, 1) for d in (1, -1)] + [sib_dev]
    partners += [z_dev(1), z_dev(-1)]
    for to in partners:
        pl.semaphore_signal(barrier, inc=1, device_id=to, device_id_type=MESH)

    own_copy = pltpu.make_async_copy(int_hbm, gath.at[p], own_sem)
    own_copy.start()
    own_amps = amps.at[pl.ds(core * (NZ * KT) + z * KT, KT)]
    for q in range(KT):
        pltpu.make_async_copy(amp_hbm.at[:, pl.ds(q * T, T)], own_amps.at[q], amp_sem).start()
    index_copies = [
        pltpu.make_async_copy(cd_hbm, cd, index_sem.at[0]), pltpu.make_async_copy(ab_hbm, ab, index_sem.at[1])
    ]
    for c in index_copies:
        c.start()
    pl.semaphore_wait(barrier, len(partners))

    SHIFT = (0, -1, 1, 2)
    FIRST, FIRST_FAR, SECOND, SECOND_FAR = 0, 1, 2, 6

    def xy_start(b, h, sem, who, to, part=None, own=False):
        start, count = pl.multiple_of(quad_of(z, b, h) * CHUNK, CHUNK), CHUNK
        if part is not None:
            start, count = start + part * PIECE, PIECE
        src = int_hbm if own else gath.at[flat(who)]
        remote(
            src.at[pl.ds(start, count)], gath.at[flat(who), pl.ds(start, count)],
            xy_send, xy_recv.at[b, sem], xy_dev(to),
        ).start()

    def xy_wait(b, sem, chunks):
        if chunks * CHUNK > SHARD:
            some = gath.at[pl.ds(0, chunks * CHUNK // SHARD)]
        else:
            some = gath.at[0, pl.ds(0, chunks * CHUNK)]
        pltpu.make_async_copy(some, some, xy_recv.at[b, sem]).wait()

    def first_own(b):
        for h in (0, 1):
            for d in (1, -1):
                xy_start(b, h, FIRST, place(h, 0, 0), place(h, d, 0), own=True)

    def second(b, q, own=False):
        for h in (0, 1):
            for d in (1, -1):
                xy_start(b, h, SECOND + q, place(h, SHIFT[q], 0), place(h, 0, d), own=own)

    def first_forward(b):
        xy_wait(b, FIRST, 4)
        for h in (0, 1):
            for d in (1, -1):
                xy_start(b, h, FIRST_FAR, place(h, -d, 0), place(h, d, 0), part=(1 - d) // 2)

    def first_far(b):
        xy_wait(b, FIRST_FAR, 2)
        second(b, 3)

    def second_forward(b, q):
        xy_wait(b, SECOND + q, 4)
        for h in (0, 1):
            for d in (1, -1):
                xy_start(b, h, SECOND_FAR, place(h, SHIFT[q], -d), place(h, 0, d), part=(1 - d) // 2)

    def second_far(b):
        xy_wait(b, SECOND_FAR, 8)

    SIGN = (1, -1)

    def tiles_wait(sem, count):
        some = amps.at[pl.ds(0, count)]
        pltpu.make_async_copy(some, some, sem).wait()

    def shard(owner_core, d):
        return amps.at[pl.ds(owner_core * (NZ * KT) + z_at(d) * KT, KT)]

    def z_start(dist, q):
        for way in (0, 1):
            part = shard(core, -SIGN[way] * (dist - 1)).at[q]
            if dist == FAR:
                part = part.at[pl.ds(way * (T // 2), T // 2)]
            remote(part, part, z_send, z_recv.at[dist - 1, q], z_dev(SIGN[way])).start()

    def to_sibling(dist):
        for way in (0,) if dist in (0, FAR) else (0, 1):
            part = shard(core, SIGN[way] * dist)
            remote(part, part, c_send, c_recv.at[0 if dist <= SOON else 1 if dist < FAR else 2], sib_dev).start()

    def from_sibling(n):
        tiles_wait(c_recv.at[n], KT * (1 + 2 * SOON, 2 * (FAR - 1 - SOON), 1)[n])

    def z_take(dist, q):
        tiles_wait(z_recv.at[dist - 1, q], 1 if dist == FAR else 2)
        if dist < FAR:
            z_start(dist + 1, q)
        if q == KT - 1:
            to_sibling(dist)

    def products(b, first, count):
        def body(n, carry):
            at = jnp.where(n < QUAD, quad_of(z, b, 0), quad_of(z, b, 1)) * QUAD + n % QUAD
            slot = n % 2 * (CORES * KT)
            for c in range(CORES):
                stage[pl.ds(slot + c * KT, KT)] = amps[pl.ds(c * (NZ * KT) + at * KT, KT)]
            for k in range(CAP):
                rows = pl.ds(pl.multiple_of(at * (2 * CAP * ROWS) + k * 2 * ROWS, 2 * ROWS), 2 * ROWS)
                group = gath[:, rows, :].astype(jnp.float32)
                for odd in (0, 1):
                    tile = group[:, odd * ROWS : (odd + 1) * ROWS, :].reshape(T, T).astype(jnp.bfloat16)
                    m = 2 * k + odd
                    which = inside(table[WHICH + m % CAP, at * CORES + m // CAP], KT)
                    prods[at * (2 * CAP) + m] = jnp.dot(
                        stage[slot + m // CAP * KT + which], tile, preferred_element_type=jnp.float32
                    )
            return carry

        lax.fori_loop(first, first + count, body, 0, unroll=count)

    def running(b):
        def body(t, acc):
            acc = jnp.where(table[KEEP, t] > 0, acc, 0.0) + prods[inside(table[PERM, t], TILES)]
            sums[t] = acc
            return acc

        lax.fori_loop(b * BATCH_TILES, (b + 1) * BATCH_TILES, body, jnp.zeros((T, T), jnp.float32), unroll=8)

    def slot_sum(b, r):
        at = b * RES + r
        return jnp.where(table[USED, at] > 0, sums[inside(table[LAST, at], TILES)], 0.0)

    def pick(b):
        def body(r, carry):
            value = slot_sum(b, r)
            own[r] = value if b == 0 else own[r] + value
            return carry

        lax.fori_loop(0, RES, body, 0, unroll=8)

    to_scalars = pltpu.make_async_copy(table_vmem, table, index_sem.at[0])

    def make_table():
        for c in index_copies:
            c.wait()
        place_table(table_vmem, cd, ab, owner, z, g)
        to_scalars.start()

    def table_done():
        to_scalars.wait()

    first_own(1)
    tiles_wait(amp_sem, KT)
    z_start(1, 0)
    first_own(0)
    z_start(1, 1)
    make_table()
    z_start(1, 2)
    second(1, 0, True)
    z_take(1, 0)
    second(0, 0, True)
    z_take(1, 1)
    z_take(1, 2)
    first_forward(0)
    second(0, 1)
    z_take(2, 0)
    first_forward(1)
    z_take(2, 1)
    second(0, 2)
    second(1, 1)
    z_take(2, 2)
    z_take(3, 0)
    first_far(0)
    z_take(3, 1)
    z_take(3, 2)
    second(1, 2)
    z_take(4, 0)
    first_far(1)
    z_take(4, 1)
    z_take(4, 2)
    z_take(5, 0)
    second_forward(0, 1)
    second_forward(0, 2)
    z_take(5, 1)
    second_forward(0, 0)
    z_take(5, 2)
    second_forward(0, 3)
    to_sibling(0)
    z_take(6, 0)
    second_forward(1, 3)
    second_forward(1, 0)
    from_sibling(0)
    z_take(6, 1)
    second_forward(1, 2)
    second_forward(1, 1)
    z_take(6, 2)
    second_far(0)
    own_copy.wait()
    table_done()
    products(0, 0, 2)
    z_take(7, 0)
    products(0, 4, 2)
    z_take(7, 1)
    products(0, 2, 2)
    z_take(7, 2)
    products(0, 6, 2)
    running(0)
    pick(0)
    second_far(1)
    z_take(8, 0)
    from_sibling(1)
    z_take(8, 1)
    z_take(8, 2)
    products(1, 0, 4)
    from_sibling(2)
    products(1, 4, 4)
    running(1)
    pick(1)

    def both(dist):
        return (0,) if dist == 0 else (dist, -dist)

    def blocks_wait(ref, sem, count):
        some = ref.at[pl.ds(0, count)]
        pltpu.make_async_copy(some, some, sem).wait()

    def cross_start(dist):
        for d in both(dist):
            remote(own.at[z_at(d) * CORES + sib], cross.at[FAR - 1 + d], x_send, x_recv.at[dist], sib_dev).start()

    def cross_wait(dist):
        blocks_wait(cross, x_recv.at[dist], len(both(dist)))

    hrows = T // PARTS

    def ring_start(way, dist, part):
        rows = pl.ds(part * hrows, hrows)
        hop = JUMP_SUM if dist == JUMP_SUM else 1
        remote(
            ring_out.at[2 * dist - 2 + way, rows], ring_in.at[2 * dist - 2 + way, rows],
            r_send, r_recv.at[dist - 1, part], z_dev(SIGN[way] * hop),
        ).start()

    def far_start(part):
        way = part % 2
        rows = pl.ds(part * hrows, hrows)
        to = z_at(SIGN[way]) * CORES
        block = z_at(FAR) * CORES
        remote(
            own.at[block + core, rows], ring_in.at[2 * FAR - 2 + way, rows],
            r_send, r_recv.at[FAR - 1, part], (p, to + core),
        ).start()
        remote(
            own.at[block + sib, rows], far_in.at[way, rows],
            r_send, r_recv.at[FAR - 1, part], (p, to + sib),
        ).start()

    def ring_wait(dist, part):
        some = ring_in.at[0, pl.ds(0, 2 * hrows)]
        pltpu.make_async_copy(some, some, r_recv.at[dist - 1, part]).wait()

    def total(d, part):
        rows = pl.ds(part * hrows, hrows)
        return own[z_at(d) * CORES + core, rows, :] + cross[FAR - 1 + d, rows, :]

    def arrived(way, dist, part):
        return ring_in[2 * dist - 2 + way, part * hrows : (part + 1) * hrows, :]

    def ring_step(dist, part):
        adds = dist != JUMP_SUM - 1
        if adds:
            ring_wait(dist + 1, part)
        for way in (0, 1):
            value = total(SIGN[way] * dist, part)
            if adds and (dist + 1 < FAR or part % 2 == way):
                value = value + arrived(way, dist + 1, part)
            if dist + 1 == FAR and part % 2 == way:
                value = value + far_in[way, part * hrows : (part + 1) * hrows, :]
            ring_out[2 * dist - 2 + way, part * hrows : (part + 1) * hrows, :] = value
            ring_start(way, dist, part)

    def finish(part):
        value = total(0, part)
        for dist in sorted({1, JUMP_SUM}):
            ring_wait(dist, part)
            for way in (0, 1):
                value = value + arrived(way, dist, part)
        out_ref[part * hrows : (part + 1) * hrows, :] = value.astype(jnp.bfloat16)

    far_start(0)
    far_start(1)
    far_start(2)
    far_start(3)
    cross_start(4)
    cross_start(7)
    cross_wait(4)
    ring_step(4, 0)
    ring_step(4, 1)
    cross_start(3)
    ring_step(4, 3)
    cross_start(6)
    cross_start(2)
    cross_start(5)
    ring_step(4, 2)
    cross_wait(7)
    cross_wait(3)
    ring_step(7, 0)
    cross_start(1)
    ring_step(3, 0)
    cross_wait(6)
    ring_step(7, 3)
    ring_step(3, 1)
    cross_wait(5)
    ring_step(7, 1)
    ring_step(3, 3)
    ring_step(7, 2)
    ring_step(3, 2)
    cross_wait(2)
    cross_start(0)
    ring_step(6, 0)
    ring_step(2, 0)
    ring_step(6, 3)
    ring_step(6, 1)
    ring_step(2, 3)
    ring_step(6, 2)
    ring_step(2, 1)
    cross_wait(0)
    ring_step(5, 0)
    ring_step(2, 2)
    ring_step(5, 3)
    ring_step(5, 1)
    ring_step(5, 2)
    cross_wait(1)
    ring_step(1, 2)
    ring_step(1, 3)
    ring_step(1, 0)
    ring_step(1, 1)
    finish(3)
    finish(0)
    finish(1)
    finish(2)

    some = gath.at[pl.ds(0, NP - 1)]
    pltpu.make_async_copy(some, some, xy_send).wait()
    tiles_wait(z_send, KT * (2 * FAR - 1))
    tiles_wait(c_send, KT * 2 * FAR)
    blocks_wait(own, x_send, NZ - 1)
    blocks_wait(ring_out, r_send, 2 * FAR)


def per_device(amplitudes, integrals, cd_index, ab_index, owner_map):
    shard = integrals.reshape(SHARD, T)
    dma = pltpu.SemaphoreType.DMA
    return pl.pallas_call(
        kernel,
        out_shape=jax.ShapeDtypeStruct((T, T), jnp.bfloat16),
        in_specs=[
            pl.BlockSpec(memory_space=pltpu.HBM),
            pl.BlockSpec(memory_space=pltpu.HBM),
            pl.BlockSpec(memory_space=pltpu.VMEM),
            pl.BlockSpec(memory_space=pltpu.HBM),
            pl.BlockSpec(memory_space=pltpu.HBM),
        ],
        out_specs=pl.BlockSpec(memory_space=pltpu.VMEM),
        scratch_shapes=[
            pltpu.SMEM((16, WIDE), jnp.int32),
            pltpu.VMEM((CAP, NI, NI), jnp.int32),
            pltpu.VMEM((CAP, NI, NI), jnp.int32),
            pltpu.VMEM((16, WIDE), jnp.int32),
            dma((2,)),
            pltpu.VMEM((NP, SHARD, T), jnp.bfloat16),
            pltpu.VMEM((CORES * NZ * KT, T, T), jnp.bfloat16),
            pltpu.VMEM((2 * CORES * KT, T, T), jnp.bfloat16),
            pltpu.VMEM((TILES, T, T), jnp.float32),
            pltpu.VMEM((TILES, T, T), jnp.float32),
            pltpu.VMEM((RES, T, T), jnp.float32),
            pltpu.VMEM((NZ - 1, T, T), jnp.float32),
            pltpu.VMEM((2, T, T), jnp.float32),
            pltpu.VMEM((2 * FAR, T, T), jnp.float32),
            pltpu.VMEM((2 * FAR, T, T), jnp.float32),
            dma, dma,
            dma, dma((BATCHES, 7)),
            dma, dma((FAR, KT)),
            dma, dma((3,)),
            dma, dma((FAR,)),
            dma, dma((FAR, PARTS)),
        ],
        compiler_params=pltpu.CompilerParams(
            collective_id=0, has_side_effects=True, vmem_limit_bytes=VMEM
        ),
        name="ladder",
    )(cd_index.transpose(2, 0, 1), ab_index.transpose(2, 0, 1), owner_map.reshape(1, RES), amplitudes, shard)


def solution(mesh):
    return jax.shard_map(
        per_device,
        mesh=mesh,
        in_specs=(P("pair", "intg"), P("intg", None, None, "pair", None), P(), P(), P()),
        out_specs=P("pair", "intg"),
        check_vma=False,
    )
```
